256 devices in a mesh: section: 16 (over y_lo, x, core), dp: 16 (over z, y_hi).
Axes of the slice: x: 4, y: 4 (y_hi: 2, y_lo: 2; y = y_hi * 2 + y_lo), z: 8, core: 2. Of those that a mesh axis runs over, the one named last changes fastest.
Arguments:
- sent_forward: bfloat16 [16, 2048, 4096], P('section', 'dp'), may hold values from -6 to 6
- sent_backward: bfloat16 [16, 2048, 4096], P('section', 'dp'), may hold values from -6 to 6
- stash_halves: bfloat16 [2, 16, 1024, 4096], P(None, 'section', 'dp'), may hold values from -6 to 6
- norm_gain: float32 [16, 4096], P('section'), may hold values from 0.1 to 1.9
- kv_weight: bfloat16 [16, 4096, 1024], P('section', 'dp'), may hold values from -1 to 6
- doc_forward: int32 [16, 2048], P('section', 'dp'), may hold values from 0 to 63, never falling along the last dimension, each value on 1 to 256 neighbouring positions
- doc_backward: int32 [16, 2048], P('section', 'dp'), may hold values from 0 to 63, never falling along the last dimension, each value on 1 to 256 neighbouring positions
Outputs:
- section_output: bfloat16 [16, 2048, 4096], P('section', 'dp')
- input_grad: bfloat16 [16, 2048, 4096], P('section', 'dp')
- parked_halves: bfloat16 [2, 16, 1024, 4096], P(None, 'section', 'dp')
- kv_grad: bfloat16 [16, 4096, 1024], P('section', 'dp')
The draws below stay inside these ranges and needn't reach their ends.
Inputs may be any that keep to these rules, and one draw needn't show every extreme that they name: `doc_forward`: document ids never fall along a row of 2048; each document spans 1 to 256 positions. `doc_backward`: document ids never fall along a row of 2048; each document spans 1 to 256 positions.
All inputs are finite; a program needn't handle non-finite values.
Results may differ from the reference program's by a relative error of at most 0.02.
Values may be sent and summed in bfloat16 or wider, within the bound.
No kernel may reach another device: no remote copies, remote signals or barrier semaphores. Data moves between devices by JAX's collectives and lax.ppermute only.
A program may use at most 128 MiB of HBM per device.

```python
import math
import jax
import jax.numpy as jnp
import numpy as np
from jax import lax

D = 4096
HEADS = 32
KV_HEADS = 4
HEAD_DIM = 128
TOK = 128
HALF = 64
KVW = 1024
SECTIONS = 16
TOKENS = 2048
N_DP = 16


def draw_sent_forward(key, part):
    key = jax.random.fold_in(key, 11)
    subkeys = jax.random.split(key, 1)
    full_shape = (SECTIONS, N_DP, TOK, D)
    values = jax.random.truncated_normal(subkeys[0], -6.0, 6.0, full_shape, jnp.float32)
    return jnp.clip(values, -6.0, 6.0).reshape(SECTIONS, TOKENS, D).astype(jnp.bfloat16)


def draw_stash_halves(key, part):
    key = jax.random.fold_in(key, 23)
    subkeys = jax.random.split(key, 2)
    full_shape = (2, SECTIONS, N_DP, HALF, D)
    values = jax.random.truncated_normal(subkeys[0], -6.0, 6.0, full_shape, jnp.float32)
    offset = jax.random.randint(subkeys[1], (), 0, N_DP)
    column_block = jnp.arange(D) // (D // N_DP)
    owners = (jnp.arange(N_DP) + offset) % N_DP
    spiked = jnp.where(column_block[None, :] == owners[:, None], 3.0, 1.0)
    values = values * spiked.reshape(1, 1, N_DP, 1, D)
    return jnp.clip(values, -6.0, 6.0).reshape(2, SECTIONS, N_DP * HALF, D).astype(jnp.bfloat16)


def draw_kv_weight(key, part):
    key = jax.random.fold_in(key, 37)
    subkeys = jax.random.split(key, 1)
    values = jax.random.truncated_normal(subkeys[0], -6.0, 6.0, (SECTIONS, D, KVW), jnp.float32) * D ** (-0.5)
    return values.astype(jnp.bfloat16)


def block_levels(rng, dims, shards, least, top_value):
    def one(dim, parts):
        steps = jax.random.uniform(jax.random.fold_in(jax.random.fold_in(rng, 6), dim), (parts,), jnp.float32, least / len(shards), top_value / len(shards))
        return jnp.repeat(jnp.exp(steps), dims[dim] // parts).reshape((-1,) + (1,) * (len(dims) - dim - 1))

    gain = one(*shards[0])
    for cut in shards[1:]:
        gain = gain * one(*cut)
    return gain


def length_profile(number_of, total, reach, skew):
    portions = [(1 << 20) // math.isqrt(standing ** skew) + 1 for standing in range(2, number_of + 1)]
    rest, given = total - reach - (number_of - 1), [1] * (number_of - 1)
    while rest > 0:
        free = [i for i in range(number_of - 1) if given[i] < reach]
        whole, remaining = sum([portions[i] for i in free]), rest
        for i in free:
            addition = min(reach - given[i], max(1, remaining * portions[i] // whole), rest)
            given[i] = given[i] + addition
            rest = rest - addition
    return np.array([reach] + given)


def ragged(rng, amount, total, bound, slope):
    if amount == 2:
        one = jax.random.randint(rng, (), max(1, total - bound), min(bound, total - 1) + 1)
        return jnp.stack([one, total - one])
    lengths = jnp.asarray(length_profile(amount, total, bound, slope), jnp.int32)
    pairs = (amount - 1) // 2
    source_of, taker = lengths[1:1 + 2 * pairs:2], lengths[2:2 + 2 * pairs:2]
    margin = jnp.minimum(source_of - 1, bound - taker)
    passed = jax.random.randint(jax.random.fold_in(rng, 1), (pairs,), 0, 1 << 20) % (margin + 1)
    lengths = lengths.at[1:1 + 2 * pairs:2].set(source_of - passed).at[2:2 + 2 * pairs:2].set(taker + passed)
    return lengths[jax.random.permutation(jax.random.fold_in(rng, 2), amount)]


def scatter_about(own_key, shape, scale, reach, cuts=(), held_as=jnp.bfloat16):
    factor_of = block_levels(own_key, shape, cuts, -0.22, 0.18) if cuts else 1.0
    array = jax.random.normal(own_key, shape, jnp.float32) * scale * factor_of
    return jnp.minimum(jnp.maximum(array, -reach), reach).astype(held_as)


def setup_inputs(seed: int = 0) -> dict:
    streams_of = jax.random.split(jax.random.key(seed), 8)
    sent_forward = draw_sent_forward(jax.random.fold_in(streams_of[7], 71), 0)
    sent_backward = scatter_about(streams_of[1], (SECTIONS, TOKENS, D), 1.0, 6.0, ((0, 16), (1, 16)))
    stash_halves = draw_stash_halves(jax.random.fold_in(streams_of[7], 71), 0)
    norm_gain = jnp.clip(1.0 + 0.18 * jax.random.normal(streams_of[3], (SECTIONS, D), jnp.float32), 0.1, 1.9)
    kv_weight = draw_kv_weight(jax.random.fold_in(streams_of[7], 71), 0)
    doc_forward = jax.vmap(lambda own: jnp.searchsorted(jnp.cumsum(ragged(own, 4 * N_DP, TOKENS, 2 * TOK, 1)), jnp.arange(TOKENS), side="right"))(jax.random.split(streams_of[5], SECTIONS)).reshape((SECTIONS, TOKENS)).astype(jnp.int32)
    doc_backward = jax.vmap(lambda own: jnp.searchsorted(jnp.cumsum(ragged(own, 4 * N_DP, TOKENS, 2 * TOK, 1)), jnp.arange(TOKENS), side="right"))(jax.random.split(streams_of[6], SECTIONS)).reshape((SECTIONS, TOKENS)).astype(jnp.int32)
    return {"sent_forward": sent_forward, "sent_backward": sent_backward, "stash_halves": stash_halves, "norm_gain": norm_gain, "kv_weight": kv_weight, "doc_forward": doc_forward, "doc_backward": doc_backward}


def normalize(wide_input, norm_scale):
    inverse = lax.rsqrt(lax.optimization_barrier(jnp.mean(wide_input * wide_input, axis=-1, keepdims=True)) + 1e-05)
    return ((wide_input * inverse * norm_scale).astype(jnp.bfloat16), inverse)

def attention_probs(normed, weight, doc_ids):
    length = normed.shape[0]
    kv_width = KV_HEADS * HEAD_DIM
    keyvals = jnp.dot(normed, weight, preferred_element_type=jnp.float32).astype(jnp.bfloat16)
    queries = normed.reshape(length, KV_HEADS, HEADS // KV_HEADS, HEAD_DIM).astype(jnp.float32)
    key_heads = keyvals[:, :kv_width].reshape(length, KV_HEADS, HEAD_DIM).astype(jnp.float32)
    value_heads = keyvals[:, kv_width:].reshape(length, KV_HEADS, HEAD_DIM).astype(jnp.float32)
    scores = jnp.einsum('qgjd,kgd->gjqk', queries, key_heads) * HEAD_DIM ** (-0.5)
    position = jnp.arange(length)
    allowed = (position[:, None] >= position[None, :]) & (doc_ids[:, None] == doc_ids[None, :])
    scores = jnp.where(allowed, scores, jnp.float32(-1e+30))
    highest = lax.optimization_barrier(jnp.max(scores, axis=-1, keepdims=True))
    powers = jnp.exp(scores - highest)
    attn_probs = powers / lax.optimization_barrier(jnp.sum(powers, axis=-1, keepdims=True))
    return (queries, key_heads, value_heads, keyvals, attn_probs)

def layer_forward(inputs, norm_scale, weight, doc_ids):
    wide_input = inputs.astype(jnp.float32)
    normed, inverse = normalize(wide_input, norm_scale)
    queries, key_heads, value_heads, keyvals, attn_probs = attention_probs(normed, weight, doc_ids)
    probs_b = attn_probs.astype(jnp.bfloat16).astype(jnp.float32)
    mixed = jnp.einsum('gjqk,kgd->qgjd', probs_b, value_heads)
    return (wide_input + mixed.reshape(inputs.shape[0], D)).astype(jnp.bfloat16)

def layer_backward(stashed, cotangent, norm_scale, weight, doc_ids):
    length = stashed.shape[0]
    wide_input = stashed.astype(jnp.float32)
    normed, inverse = normalize(wide_input, norm_scale)
    queries, key_heads, value_heads, keyvals, attn_probs = attention_probs(normed, weight, doc_ids)
    probs_b = attn_probs.astype(jnp.bfloat16).astype(jnp.float32)
    head_grad = cotangent.reshape(length, KV_HEADS, HEADS // KV_HEADS, HEAD_DIM).astype(jnp.float32)
    value_grad = jnp.einsum('gjqk,qgjd->kgd', probs_b, head_grad)
    prob_grad = jnp.einsum('qgjd,kgd->gjqk', head_grad, value_heads)
    centre = lax.optimization_barrier(jnp.sum(attn_probs * prob_grad, axis=-1, keepdims=True))
    score_grad = (attn_probs * (prob_grad - centre) * HEAD_DIM ** (-0.5)).astype(jnp.bfloat16).astype(jnp.float32)
    query_grad = jnp.einsum('gjqk,kgd->qgjd', score_grad, key_heads).reshape(length, D)
    key_grad = jnp.einsum('gjqk,qgjd->kgd', score_grad, queries)
    kv_cotan = jnp.concatenate([key_grad.reshape(length, -1), value_grad.reshape(length, -1)], axis=-1).astype(jnp.bfloat16)
    normed_grad = query_grad + jnp.dot(kv_cotan, weight.T, preferred_element_type=jnp.float32)
    scaled_grad = normed_grad * norm_scale
    moment = lax.optimization_barrier(jnp.mean(scaled_grad * wide_input, axis=-1, keepdims=True))
    result = cotangent.astype(jnp.float32) + inverse * scaled_grad - wide_input * inverse ** 3 * moment
    return (result.astype(jnp.bfloat16), kv_cotan, normed)

def reference(sent_forward, sent_backward, stash_halves, norm_gain, kv_weight, doc_forward, doc_backward):
    sections = sent_forward.shape[0]
    incoming = jnp.roll(sent_forward, 1, axis=0).reshape(sections, N_DP, TOK, D)
    cotangent = jnp.roll(sent_backward, -1, axis=0).reshape(sections, N_DP, TOK, D)
    halves = stash_halves.reshape(2, sections, N_DP, HALF, D)
    stashed = jnp.concatenate([halves[0], halves[1][::-1]], axis=2)
    parked = jnp.stack([incoming[:, :, :HALF], incoming[:, :, HALF:][::-1]]).reshape(2, sections, N_DP * HALF, D)
    ids_forward = doc_forward.reshape(sections, N_DP, TOK)
    ids_backward = doc_backward.reshape(sections, N_DP, TOK)

    def one_section(inputs):
        arriving, returning, earlier, norm_scale, weight, first_ids, second_ids = inputs
        layer_out = jax.vmap(layer_forward, (0, None, None, 0))(arriving, norm_scale, weight, first_ids)
        back_grad, kv_cotan, normed = jax.vmap(layer_backward, (0, 0, None, None, 0))(earlier, returning, norm_scale, weight, second_ids)
        weight_grad = jnp.dot(normed.reshape(-1, D).T, kv_cotan.reshape(-1, KVW), preferred_element_type=jnp.float32)
        return (layer_out, back_grad, weight_grad.astype(jnp.bfloat16))
    layer_out, back_grad, weight_grad = lax.map(one_section, (incoming, cotangent, stashed, norm_gain, kv_weight, ids_forward, ids_backward))
    return (layer_out.reshape(sections, N_DP * TOK, D), back_grad.reshape(sections, N_DP * TOK, D), parked, weight_grad)
```

```python
import functools
import math

import jax
import jax.numpy as jnp
from jax import lax
from jax.experimental import pallas as pl
from jax.experimental.pallas import tpu as pltpu
from jax.sharding import PartitionSpec as P

HEADS = 32
KV_HEADS = 4
GROUP = HEADS // KV_HEADS
HEAD_DIM = 128
SCALE = HEAD_DIM ** (-0.5)
F32 = jnp.float32
BF16 = jnp.bfloat16
VMEM = pl.BlockSpec(memory_space=pltpu.VMEM)
SMEM = pl.BlockSpec(memory_space=pltpu.SMEM)


def struct(shape, dtype):
    return jax.ShapeDtypeStruct(shape, dtype)


def call(body, name, outs, args, scratch=(), flops=0, moved=0, exps=0, limit=40):
    return pl.pallas_call(
        body,
        name=name,
        out_shape=outs,
        in_specs=[SMEM] + [VMEM] * (len(args) - 1),
        out_specs=jax.tree.map(lambda _: VMEM, outs),
        scratch_shapes=scratch,
        cost_estimate=pl.CostEstimate(flops=flops, bytes_accessed=moved, transcendentals=exps),
        compiler_params=pltpu.CompilerParams(vmem_limit_bytes=limit * 2**20),
    )(*args)


def columns(index, width):
    return pl.ds(pl.multiple_of(index * width, width), width)


def nt(a, b):
    return lax.dot_general(a, b, (((1,), (1,)), ((), ())), preferred_element_type=F32)


def tn(a, b):
    return lax.dot_general(a, b, (((0,), (0,)), ((), ())), preferred_element_type=F32)


def nn(a, b):
    return jnp.dot(a, b, preferred_element_type=F32)


def norm_rows(x, gain):
    wide = x.astype(F32)
    inverse = lax.rsqrt(jnp.mean(wide * wide, axis=-1, keepdims=True) + 1e-05)
    return (wide * inverse * gain).astype(BF16), inverse


def norm_body(parts, pos, *refs):
    inputs, gain, normed, inverse, blocks = refs[:parts], refs[parts], refs[parts + 1], refs[parts + 2], refs[parts + 3 :]
    step = 32
    row = 0
    for x in inputs:
        for part in range(0, x.shape[0], step):
            out, inv = norm_rows(x[pl.ds(part, step), :], gain[...])
            normed[pl.ds(row, step), :] = out
            inverse[pl.ds(row, step), :] = jnp.broadcast_to(inv, (step, 128))
            row += step
    for away, block in enumerate(blocks):
        width = block.shape[1]
        block[...] = normed[:, columns(lax.rem(pos[0] + away, len(blocks)), width)]


def rows_of(pos, place, n_z):
    dz, dy, part, parts = place
    owner = lax.rem(pos[0] + dz, n_z) * 2 + (pos[1] if dy == 0 else 1 - pos[1])
    return owner * parts + part


def project_body(places, n_z, pos, back, ahead, *refs):
    pieces, kv_back, kv_ahead, rows, total = refs[:-4], refs[-4], refs[-3], refs[-2], refs[-1]
    length = back.shape[0]
    rows[:length, :] = back[...]
    rows[length:, :] = ahead[...]
    for i, (place, piece) in enumerate(zip(places, pieces)):
        part = nn(rows[:, columns(rows_of(pos, place, n_z), piece.shape[0])], piece[...])
        if i == 0:
            total[...] = part
        elif i < len(pieces) - 1:
            total[...] += part
        else:
            kv_back[...] = (total[:length, :] + part[:length, :]).astype(BF16)
            kv_ahead[...] = (total[length:, :] + part[length:, :]).astype(BF16)


def mask_of(doc):
    length = doc.shape[1]
    across = jnp.broadcast_to(doc.astype(F32), (length, length))
    query = lax.broadcasted_iota(jnp.int32, (length, length), 0)
    key = lax.broadcasted_iota(jnp.int32, (length, length), 1)
    return (query >= key) & (across == across.T)


def probs_of(query, key, mask):
    scores = jnp.where(mask, nt(query, key), F32(-1e30))
    highest = jnp.max(scores, axis=-1, keepdims=True)
    powers = jnp.exp2((scores - highest) * F32(SCALE * math.log2(math.e)))
    return powers * (1.0 / jnp.sum(powers, axis=-1, keepdims=True))


def head(i):
    return pl.ds(i * HEAD_DIM, HEAD_DIM)


def back_attention_body(pos, doc, normed, kv, cotangent, kv_cotan, score_grads):
    mask = mask_of(doc[...])
    for group in range(KV_HEADS):
        key, value = kv[:, head(group)], kv[:, head(KV_HEADS + group)]
        key_grad = value_grad = None
        for j in range(group * GROUP, (group + 1) * GROUP):
            query, grad = normed[:, head(j)], cotangent[:, head(j)]
            probs = probs_of(query, key, mask)
            prob_grad = nt(grad, value)
            centre = jnp.sum(probs * prob_grad, axis=-1, keepdims=True)
            score_grad = (probs * (prob_grad - centre) * F32(SCALE)).astype(BF16)
            score_grads[:, head(j)] = score_grad
            one_value = tn(probs.astype(BF16), grad)
            one_key = tn(score_grad, query)
            value_grad = one_value if value_grad is None else value_grad + one_value
            key_grad = one_key if key_grad is None else key_grad + one_key
        kv_cotan[:, head(group)] = key_grad.astype(BF16)
        kv_cotan[:, head(KV_HEADS + group)] = value_grad.astype(BF16)


def ahead_attention_body(pos, doc, normed, kv, incoming, evicted, out, parked):
    mask = mask_of(doc[...])
    half = evicted.shape[0]
    parked[0, 0] = incoming[:half, :]
    parked[1, 0] = evicted[...]
    for j in range(HEADS):
        group = j // GROUP
        probs = probs_of(normed[:, head(j)], kv[:, head(group)], mask).astype(BF16)
        mixed = nn(probs, kv[:, head(KV_HEADS + group)])
        out[0, :, head(j)] = (incoming[:, head(j)].astype(F32) + mixed).astype(BF16)


def input_grad_body(
    places, n_z, pos, score_grads, kv, kv_cotan, first, second, inverse, gain, cotangent, *refs
):
    pieces, out, grads = refs[:-2], refs[-2], refs[-1]
    for place, piece in zip(places, pieces):
        grads[:, columns(rows_of(pos, place, n_z), piece.shape[0])] = nt(kv_cotan[...], piece[...])
    half, width = first.shape
    for j in range(HEADS):
        grads[:, head(j)] += nn(score_grads[:, head(j)], kv[:, head(j // GROUP)])
    step = 32
    for row in range(0, 2 * half, step):
        source, at = (first, row) if row < half else (second, row - half)
        wide = source[pl.ds(at, step), :].astype(F32)
        scaled = grads[pl.ds(row, step), :] * gain[...]
        moment = jnp.mean(scaled * wide, axis=-1, keepdims=True)
        inv = inverse[pl.ds(row, step), :1]
        total = cotangent[pl.ds(row, step), :].astype(F32) + inv * scaled - wide * (inv * inv * inv * moment)
        out[0, pl.ds(row, step), :] = total.astype(BF16)


def kv_grad_body(other, n, pos, *refs):
    lefts, rights, out = refs[:n], refs[n : 2 * n], refs[-1]
    width = out.shape[0]
    place = 1 - pos[1] if other else pos[1]
    left = jnp.concatenate([ref[:, columns(place, width)] for ref in lefts], axis=0)
    right = jnp.concatenate([ref[...] for ref in rights], axis=0)
    out[...] = tn(left, right).astype(out.dtype)


def add_body(pos, mine, theirs, out):
    out[0] = (mine[...] + theirs[...].astype(F32)).astype(BF16)


def section_permute(value, to):
    n = lax.axis_size("section")
    return lax.ppermute(value, "section", [(i, to(i) % n) for i in range(n)])


def dp_permute(value, dz=0, dy=0):
    n_z = lax.axis_size("dp") // 2
    pairs = [(i, ((i // 2 + dz) % n_z) * 2 + ((i % 2) ^ dy)) for i in range(2 * n_z)]
    return lax.ppermute(value, "dp", pairs)


def ring(block, n_z, dy=0):
    got = [(block, (0, dy, 0, 1))]
    right = left = block
    for step in range(1, n_z // 2):
        right, left = dp_permute(right, dz=1), dp_permute(left, dz=-1)
        got += [(right, (n_z - step, dy, 0, 1)), (left, (step, dy, 0, 1))]
    half = block.shape[0] // 2
    got.append((dp_permute(right[:half], dz=1), (n_z // 2, dy, 0, 2)))
    got.append((dp_permute(left[half:], dz=-1), (n_z // 2, dy, 1, 2)))
    return got


def local(
    sent_forward, sent_backward, stash_halves, norm_gain, kv_weight, doc_forward, doc_backward
):
    n_dp = lax.axis_size("dp")
    n_z = n_dp // 2
    index = lax.axis_index("dp")
    pos = jnp.stack([index // 2, index % 2]).astype(jnp.int32)
    half, width = stash_halves.shape[2:]
    length = 2 * half
    weight = kv_weight[0]
    kv_width = weight.shape[1]

    first = stash_halves[0, 0]
    last = lax.axis_size("section") - 1
    second = section_permute(stash_halves[1, 0], lambda i: last - i)
    cotangent = section_permute(sent_backward, lambda i: i - 1)[0]
    incoming = section_permute(sent_forward, lambda i: i + 1)[0]
    evicted = section_permute(sent_forward[0, half:], lambda i: last - 1 - i)

    partner = dp_permute(weight, dy=1)
    gathered = ring(weight, n_z) + ring(partner, n_z, dy=1)
    pieces, places = [p for p, _ in gathered], tuple(q for _, q in gathered)

    piece_width = 2 * weight.shape[0]
    normed_back, inverse, *blocks = call(
        functools.partial(norm_body, 2),
        "norm_back",
        [struct((length, width), BF16), struct((length, 128), F32)]
        + [struct((length, piece_width), BF16)] * n_z,
        [pos, first, second, norm_gain],
        flops=6 * length * width,
        moved=6 * length * width,
    )
    normed_ahead, _ = call(
        functools.partial(norm_body, 1),
        "norm_ahead",
        [struct((length, width), BF16), struct((length, 128), F32)],
        [pos, incoming, norm_gain],
        flops=6 * length * width,
        moved=4 * length * width,
    )
    lefts = {0: blocks[0]}
    for away in range(1, n_z):
        lefts[n_z - away] = dp_permute(blocks[away], dz=away)

    kv_back, kv_ahead = call(
        functools.partial(project_body, places, n_z),
        "project",
        [struct((length, kv_width), BF16)] * 2,
        [pos, normed_back, normed_ahead] + pieces,
        scratch=[pltpu.VMEM((2 * length, width), BF16), pltpu.VMEM((2 * length, kv_width), F32)],
        flops=4 * length * width * kv_width,
        moved=2 * width * kv_width,
    )
    kv_cotan, score_grads = call(
        back_attention_body,
        "back_attention",
        [struct((length, kv_width), BF16), struct((length, width), BF16)],
        [pos, doc_backward, normed_back, kv_back, cotangent],
        flops=10 * length * length * width,
        moved=6 * length * width,
        exps=length * length * HEADS,
    )
    spread = ring(kv_cotan, n_z)
    out, parked = call(
        ahead_attention_body,
        "ahead_attention",
        [struct((1, length, width), BF16), struct((2, 1, half, width), BF16)],
        [pos, doc_forward, normed_ahead, kv_ahead, incoming, evicted],
        flops=4 * length * length * width,
        moved=8 * length * width,
        exps=length * length * HEADS,
    )
    input_grad = call(
        functools.partial(input_grad_body, places, n_z),
        "input_grad",
        struct((1, length, width), BF16),
        [pos, score_grads, kv_back, kv_cotan, first, second, inverse, norm_gain, cotangent] + pieces,
        scratch=[pltpu.VMEM((length, width), F32)],
        flops=2 * length * width * (kv_width + length),
        moved=2 * width * kv_width + 8 * length * width,
    )

    by_z = {}
    for piece, (dz, _, part, _) in spread:
        by_z.setdefault(dz, {})[part] = piece
    order = sorted(by_z)
    rights = [by_z[dz][part] for dz in order for part in sorted(by_z[dz])]
    left_list = []
    for dz in order:
        parts = len(by_z[dz])
        rows = length // parts
        left_list += [lefts[dz][i * rows : (i + 1) * rows] for i in range(parts)]
    own_rows = weight.shape[0]

    def kv_part(other, dtype):
        return call(
            functools.partial(kv_grad_body, other, len(rights)),
            "kv_grad_other" if other else "kv_grad_own",
            struct((own_rows, kv_width), dtype),
            [pos] + left_list + rights,
            flops=2 * own_rows * kv_width * length * n_z,
            moved=2 * length * n_z * (kv_width + own_rows),
        )

    theirs = dp_permute(kv_part(True, BF16), dy=1)
    mine = kv_part(False, F32)
    kv_grad = call(
        add_body,
        "kv_add",
        struct((1, own_rows, kv_width), BF16),
        [pos, mine, theirs],
        flops=own_rows * kv_width,
        moved=8 * own_rows * kv_width,
    )
    return out, input_grad, parked, kv_grad


def solution(mesh):
    return jax.shard_map(
        local,
        mesh=mesh,
        in_specs=(
            P("section", "dp", None),
            P("section", "dp", None),
            P(None, "section", "dp", None),
            P("section", None),
            P("section", "dp", None),
            P("section", "dp"),
            P("section", "dp"),
        ),
        out_specs=(
            P("section", "dp", None),
            P("section", "dp", None),
            P(None, "section", "dp", None),
            P("section", "dp", None),
        ),
        check_vma=False,
    )
```

```python
import functools
import math

import jax
import jax.numpy as jnp
from jax import lax
from jax.experimental import pallas as pl
from jax.experimental.pallas import tpu as pltpu
from jax.sharding import PartitionSpec as P

HEADS = 32
KV_HEADS = 4
GROUP = HEADS // KV_HEADS
HEAD_DIM = 128
SCALE = HEAD_DIM ** (-0.5)
F32 = jnp.float32
BF16 = jnp.bfloat16
VMEM = pl.BlockSpec(memory_space=pltpu.VMEM)
HBM = pl.BlockSpec(memory_space=pltpu.HBM)
SMEM = pl.BlockSpec(memory_space=pltpu.SMEM)


def struct(shape, dtype):
    return jax.ShapeDtypeStruct(shape, dtype)


def call(body, name, outs, args, pieces=(), scratch=(), flops=0, moved=0, exps=0, limit=40):
    return pl.pallas_call(
        body,
        name=name,
        out_shape=outs,
        in_specs=[SMEM] + [VMEM] * (len(args) - 1) + [HBM] * len(pieces),
        out_specs=jax.tree.map(lambda _: VMEM, outs),
        scratch_shapes=scratch,
        cost_estimate=pl.CostEstimate(flops=flops, bytes_accessed=moved, transcendentals=exps),
        compiler_params=pltpu.CompilerParams(vmem_limit_bytes=limit * 2**20),
    )(*args, *pieces)


def columns(index, width):
    return pl.ds(pl.multiple_of(index * width, width), width)


def nt(a, b):
    return lax.dot_general(a, b, (((1,), (1,)), ((), ())), preferred_element_type=F32)


def tn(a, b):
    return lax.dot_general(a, b, (((0,), (0,)), ((), ())), preferred_element_type=F32)


def nn(a, b):
    return jnp.dot(a, b, preferred_element_type=F32)


def norm_rows(x, gain):
    wide = x.astype(F32)
    inverse = lax.rsqrt(jnp.mean(wide * wide, axis=-1, keepdims=True) + 1e-05)
    return (wide * inverse * gain).astype(BF16), inverse


def norm_into(inputs, gain, normed, inverse):
    step, row = 32, 0
    for x in inputs:
        for part in range(0, x.shape[0], step):
            out, inv = norm_rows(x[pl.ds(part, step), :], gain[...])
            normed[pl.ds(row, step), :] = out
            inverse[pl.ds(row, step), :] = jnp.broadcast_to(inv, (step, 128))
            row += step


def norm_ahead_body(pos, x, gain, normed, inverse):
    norm_into([x], gain, normed, inverse)


def norm_back_body(n_z, carry, pos, first, second, gain, partner, normed, inverse, own, right, left):
    norm_into([first, second], gain, normed, inverse)
    half, kv_width = first.shape[0], partner.shape[1]
    part = kv_width // 2

    def place(ref, row, away, begin=0, size=half):
        cols = columns(lax.rem(pos[0] + away, n_z), part)
        ref[pl.ds(row, size), :part] = normed[pl.ds(begin, size), cols]
        ref[pl.ds(row, size), part:] = normed[pl.ds(half + begin, size), cols]

    place(own, 0, 0)
    quarter = half // 2
    for ref, sign in ((right, 1), (left, -1)):
        place(ref, 0, n_z // 2, 0 if sign == 1 else quarter, quarter)
        row = quarter
        for away in range(n_z // 2 - 1, 0, -1):
            if away == carry:
                ref[pl.ds(row, partner.shape[0]), :] = partner[...]
                row += partner.shape[0]
            place(ref, row, (sign * away) % n_z)
            row += half


def rows_of(pos, place, n_z):
    dz, dy, part, parts = place
    owner = lax.rem(pos[0] + dz, n_z) * 2 + (pos[1] if dy == 0 else 1 - pos[1])
    return owner * parts + part


def fetch(pieces, held, sems):
    started, row = [], 0
    for i, (piece, (begin, size, place)) in enumerate(pieces):
        at = held.at[pl.ds(row, size), :]
        copy = pltpu.make_async_copy(piece.at[pl.ds(begin, size), :], at, sems.at[i])
        copy.start()
        started.append((place, at, copy))
        row += size
    return started


def held_rows(pieces):
    return sum(segment[1] for _, segment in pieces)


def project_body(places, n_z, begin, finish, pos, back, ahead, *refs):
    count = len(places)
    earlier, refs = (None, refs) if begin else (refs[0], refs[1:])
    pieces, outs = refs[:count], refs[count:-4]
    rows, total, held, sems = refs[-4:]
    started = fetch(list(zip(pieces, places)), held, sems)
    length = back.shape[0]
    rows[:length, :] = back[...]
    rows[length:, :] = ahead[...]
    if earlier is not None:
        total[...] = earlier[...]
    for i, (place, at, copy) in enumerate(started):
        copy.wait()
        part = nn(rows[:, columns(rows_of(pos, place, n_z), at.shape[0])], at[...])
        if i == 0 and begin:
            total[...] = part
        elif i < count - 1:
            total[...] += part
        elif finish:
            kv_back, kv_ahead = outs
            kv_back[...] = (total[:length, :] + part[:length, :]).astype(BF16)
            kv_ahead[...] = (total[length:, :] + part[length:, :]).astype(BF16)
        else:
            outs[0][...] = total[...] + part


def mask_of(doc):
    length = doc.shape[1]
    across = jnp.broadcast_to(doc.astype(F32), (length, length))
    query = lax.broadcasted_iota(jnp.int32, (length, length), 0)
    key = lax.broadcasted_iota(jnp.int32, (length, length), 1)
    return (query >= key) & (across == across.T)


def probs_of(query, key, mask):
    scores = jnp.where(mask, nt(query, key), F32(-1e30))
    highest = jnp.max(scores, axis=-1, keepdims=True)
    powers = jnp.exp2((scores - highest) * F32(SCALE * math.log2(math.e)))
    return powers * (1.0 / jnp.sum(powers, axis=-1, keepdims=True))


def head(i):
    return pl.ds(i * HEAD_DIM, HEAD_DIM)


def stacked(ref, group):
    return jnp.concatenate([ref[:, head(group * GROUP + j)] for j in range(GROUP)], axis=0)


def back_attention_body(pos, doc, normed, kv, cotangent, kv_cotan, score_grads):
    length = normed.shape[0]
    mask = jnp.concatenate([mask_of(doc[...])] * GROUP, axis=0)
    for group in range(KV_HEADS):
        key, value = kv[:, head(group)], kv[:, head(KV_HEADS + group)]
        query, grad = stacked(normed, group), stacked(cotangent, group)
        probs = probs_of(query, key, mask)
        prob_grad = nt(grad, value)
        centre = jnp.sum(probs * prob_grad, axis=-1, keepdims=True)
        score_grad = (probs * (prob_grad - centre) * F32(SCALE)).astype(BF16)
        for j in range(GROUP):
            score_grads[:, head(group * GROUP + j)] = score_grad[j * length : (j + 1) * length]
        kv_cotan[:, head(group)] = tn(score_grad, query).astype(BF16)
        kv_cotan[:, head(KV_HEADS + group)] = tn(probs.astype(BF16), grad).astype(BF16)


def ahead_attention_body(pos, doc, normed, kv, incoming, evicted, out, parked):
    length = normed.shape[0]
    mask = jnp.concatenate([mask_of(doc[...])] * GROUP, axis=0)
    half = evicted.shape[0]
    parked[0, 0] = incoming[:half, :]
    parked[1, 0] = evicted[...]
    for group in range(KV_HEADS):
        probs = probs_of(stacked(normed, group), kv[:, head(group)], mask).astype(BF16)
        mixed = nn(probs, kv[:, head(KV_HEADS + group)])
        for j in range(GROUP):
            at = head(group * GROUP + j)
            total = incoming[:, at].astype(F32) + mixed[j * length : (j + 1) * length]
            out[0, :, at] = total.astype(BF16)


def input_grad_body(
    places, n_z, pos, score_grads, kv, kv_cotan, first, second, inverse, gain, cotangent, *refs
):
    pieces, (out, grads, held, sems) = refs[:-4], refs[-4:]
    started = fetch(list(zip(pieces, places)), held, sems)
    half, width = first.shape
    for group in range(KV_HEADS):
        key = kv[:, head(group)]
        for j in range(GROUP):
            at = head(group * GROUP + j)
            grads[:, at] = nn(score_grads[:, at], key)
    for _, _, copy in started:
        copy.wait()
    for place, at, _ in started:
        grads[:, columns(rows_of(pos, place, n_z), at.shape[0])] += nt(kv_cotan[...], at[...])
    step = 32
    for row in range(0, 2 * half, step):
        source, at = (first, row) if row < half else (second, row - half)
        wide = source[pl.ds(at, step), :].astype(F32)
        scaled = grads[pl.ds(row, step), :] * gain[...]
        moment = jnp.mean(scaled * wide, axis=-1, keepdims=True)
        inv = inverse[pl.ds(row, step), :1]
        total = cotangent[pl.ds(row, step), :].astype(F32) + inv * scaled - wide * (inv * inv * inv * moment)
        out[0, pl.ds(row, step), :] = total.astype(BF16)


def collect_body(moves, pos, *refs):
    sources, out, sems = refs[:-2], refs[-2], refs[-1]
    part = out.shape[1]
    copies = []
    for i, (source, begin, row, size, side) in enumerate(moves):
        copies.append(
            pltpu.make_async_copy(
                sources[source].at[pl.ds(begin, size), pl.ds(side * part, part)],
                out.at[pl.ds(row, size), :],
                sems.at[i],
            )
        )
        copies[-1].start()
    for copy in copies:
        copy.wait()


def kv_grad_body(other, pos, left, *refs):
    rights, out = refs[:-1], refs[-1]
    place = 1 - pos[1] if other else pos[1]
    right = jnp.concatenate([ref[...] for ref in rights], axis=0)
    out[...] = tn(left[:, columns(place, out.shape[0])], right).astype(out.dtype)


def add_body(pos, mine, theirs, out):
    out[0] = (mine[...] + theirs[...].astype(F32)).astype(BF16)


def section_permute(value, to):
    n = lax.axis_size("section")
    return lax.ppermute(value, "section", [(i, to(i) % n) for i in range(n)])


def dp_permute(value, dz=0, dy=0):
    n_z = lax.axis_size("dp") // 2
    pairs = [(i, ((i // 2 + dz) % n_z) * 2 + ((i % 2) ^ dy)) for i in range(2 * n_z)]
    return lax.ppermute(value, "dp", pairs)


def ring(block, n_z, dy=0):
    got = [(block, (0, dy, 0, 1))]
    right = left = block
    for step in range(1, n_z // 2):
        right, left = dp_permute(right, dz=1), dp_permute(left, dz=-1)
        got += [(right, (n_z - step, dy, 0, 1)), (left, (step, dy, 0, 1))]
    half = block.shape[0] // 2
    got.append((dp_permute(right[:half], dz=1), (n_z // 2, dy, 0, 2)))
    got.append((dp_permute(left[half:], dz=-1), (n_z // 2, dy, 1, 2)))
    return got


def settle(value):
    return lax.optimization_barrier(value)


def tie(value, *others):
    return lax.optimization_barrier((value,) + others)[0]


def local(
    sent_forward, sent_backward, stash_halves, norm_gain, kv_weight, doc_forward, doc_backward
):
    n_dp = lax.axis_size("dp")
    n_z = n_dp // 2
    index = lax.axis_index("dp")
    pos = jnp.stack([index // 2, index % 2]).astype(jnp.int32)
    half, width = stash_halves.shape[2:]
    length = 2 * half
    weight = kv_weight[0]
    kv_width = weight.shape[1]

    last = lax.axis_size("section") - 1
    first = stash_halves[0, 0]
    piece_width = 2 * weight.shape[0]
    mid = weight.shape[0] // 2

    carry = 1

    def both(to_right, to_left):
        return dp_permute(to_right, dz=1), dp_permute(to_left, dz=-1)

    def over(pair):
        return tuple(settle(dp_permute(value, dy=1)) for value in pair)

    partner = settle(dp_permute(weight, dy=1))
    second = section_permute(tie(stash_halves[1, 0], partner), lambda i: last - i)
    rows, quarter = weight.shape[0], half // 2
    message = struct((quarter + (n_z // 2 - 1) * half + rows, kv_width), BF16)
    normed_back, inverse, own, *messages = call(
        functools.partial(norm_back_body, n_z, carry),
        "norm_back",
        [struct((length, width), BF16), struct((length, 128), F32), struct((half, kv_width), BF16)]
        + [message] * 2,
        [pos, first, second, norm_gain, partner],
        flops=6 * length * width,
        limit=12,
        moved=6 * length * width,
    )
    early = [(weight, (0, rows, (0, 0, 0, 1))), (partner, (0, rows, (0, 1, 0, 1)))]
    late, overs = [], []
    around = (weight, weight)
    for step in range(1, n_z // 2):
        around = both(*around)
        for value, dz in zip(around, (n_z - step, step)):
            early.append((value, (0, rows, (dz, 0, 0, 1))))
        if step < 3:
            around = tuple(tie(value, partner if step == 1 else inverse) for value in around)
        if step > carry:
            overs.append(over(around))
            for value, dz in zip(overs[-1], (n_z - step, step)):
                late.append((value, (0, rows, (dz, 1, 0, 1))))
        if step == 2:
            incoming = section_permute(tie(sent_forward, *around), lambda i: i + 1)[0]
    far = both(around[0][:mid], around[1][mid:])
    cotangent = section_permute(tie(sent_backward, *around), lambda i: i - 1)[0]
    overs.append(over(far))
    for dy, pair in enumerate((far, overs[-1])):
        for part, value in enumerate(pair):
            late.append((value, (0, mid, (n_z // 2, dy, part, 2))))
    evicted = section_permute(sent_forward[0, half:], lambda i: last - 1 - i)
    sources = [own]
    moves = [(0, 0, 0, half, 0), (0, 0, half, half, 1)]
    before = {2: [incoming], 3: [cotangent] + [value for pair in overs[:-2] for value in pair], 4: list(overs[-2])}
    for step in range(1, n_z // 2 + 1):
        size = quarter + (n_z // 2 - step) * half + (rows if step <= carry else 0)
        messages = both(*(tie(value[:size], *before.get(step, [])) for value in messages))
        for value, dz, part in zip(messages, (n_z - step, step), (0, 1)):
            if step <= carry:
                begin = quarter + (n_z // 2 - 1 - carry) * half
                late.append((value, (begin, rows, (dz, 1, 0, 1))))
            at = len(sources)
            sources.append(value)
            for side in range(2):
                if step == n_z // 2:
                    moves.append((at, 0, dz * length + side * half + part * quarter, quarter, side))
                else:
                    moves.append((at, value.shape[0] - half, dz * length + side * half, half, side))
    collected = call(
        functools.partial(collect_body, moves),
        "collect",
        struct((n_z * length, kv_width // 2), BF16),
        [pos],
        sources,
        scratch=[pltpu.SemaphoreType.DMA((len(moves),))],
        limit=6,
        moved=4 * length * width,
    )

    normed_ahead, _ = call(
        norm_ahead_body,
        "norm_ahead",
        [struct((length, width), BF16), struct((length, 128), F32)],
        [pos, incoming, norm_gain],
        flops=6 * length * width,
        limit=10,
        moved=4 * length * width,
    )


    def project(some, outs, total=None, finish=False):
        return call(
            functools.partial(project_body, tuple(q for _, q in some), n_z, total is None, finish),
            "project_late" if finish else "project_early",
            outs,
            [pos, normed_back, normed_ahead] + ([] if total is None else [total]),
            [p for p, _ in some],
            scratch=[
                pltpu.VMEM((2 * length, width), BF16),
                pltpu.VMEM((2 * length, kv_width), F32),
                pltpu.VMEM((held_rows(some), kv_width), BF16),
                pltpu.SemaphoreType.DMA((len(some),)),
            ],
            flops=2 * length * width * kv_width,
            limit=20,
            moved=width * kv_width,
        )

    total = project(early, struct((2 * length, kv_width), F32))
    kv_back, kv_ahead = project(
        late, [struct((length, kv_width), BF16)] * 2, total, True
    )
    kv_cotan, score_grads = call(
        back_attention_body,
        "back_attention",
        [struct((length, kv_width), BF16), struct((length, width), BF16)],
        [pos, doc_backward, normed_back, kv_back, cotangent],
        flops=10 * length * length * width,
        limit=12,
        moved=6 * length * width,
        exps=length * length * HEADS,
    )
    spread = ring(kv_cotan, n_z)
    out, parked = call(
        ahead_attention_body,
        "ahead_attention",
        [struct((1, length, width), BF16), struct((2, 1, half, width), BF16)],
        [pos, doc_forward, normed_ahead, kv_ahead, incoming, evicted],
        flops=4 * length * length * width,
        limit=12,
        moved=8 * length * width,
        exps=length * length * HEADS,
    )
    input_grad = call(
        functools.partial(input_grad_body, tuple(q for _, q in early + late), n_z),
        "input_grad",
        struct((1, length, width), BF16),
        [pos, score_grads, kv_back, kv_cotan, first, second, inverse, norm_gain, cotangent],
        [p for p, _ in early + late],
        scratch=[
            pltpu.VMEM((length, width), F32),
            pltpu.VMEM((held_rows(early + late), kv_width), BF16),
            pltpu.SemaphoreType.DMA((len(early + late),)),
        ],
        flops=2 * length * width * (kv_width + length),
        limit=22,
        moved=2 * width * kv_width + 8 * length * width,
    )

    by_z = {}
    for piece, (dz, _, part, _) in spread:
        by_z.setdefault(dz, {})[part] = piece
    order = sorted(by_z)
    rights = [by_z[dz][part] for dz in order for part in sorted(by_z[dz])]
    own_rows = weight.shape[0]

    def kv_part(other, dtype):
        return call(
            functools.partial(kv_grad_body, other),
            "kv_grad_other" if other else "kv_grad_own",
            struct((own_rows, kv_width), dtype),
            [pos, collected] + rights,
            flops=2 * own_rows * kv_width * length * n_z,
            limit=12,
            moved=2 * length * n_z * (kv_width + own_rows),
        )

    theirs = dp_permute(kv_part(True, BF16), dy=1)
    mine = kv_part(False, F32)
    kv_grad = call(
        add_body,
        "kv_add",
        struct((1, own_rows, kv_width), BF16),
        [pos, mine, theirs],
        flops=own_rows * kv_width,
        limit=6,
        moved=8 * own_rows * kv_width,
    )
    return out, input_grad, parked, kv_grad


def solution(mesh):
    return jax.shard_map(
        local,
        mesh=mesh,
        in_specs=(
            P("section", "dp", None),
            P("section", "dp", None),
            P(None, "section", "dp", None),
            P("section", None),
            P("section", "dp", None),
            P("section", "dp"),
            P("section", "dp"),
        ),
        out_specs=(
            P("section", "dp", None),
            P("section", "dp", None),
            P(None, "section", "dp", None),
            P("section", "dp", None),
        ),
        check_vma=False,
    )
```

```python
import functools
import math

import jax
import jax.numpy as jnp
from jax import lax
from jax.experimental import pallas as pl
from jax.experimental.pallas import tpu as pltpu
from jax.sharding import PartitionSpec as P

HEADS = 32
KV_HEADS = 4
GROUP = HEADS // KV_HEADS
HEAD_DIM = 128
SCALE = HEAD_DIM ** (-0.5)
F32 = jnp.float32
BF16 = jnp.bfloat16
VMEM = pl.BlockSpec(memory_space=pltpu.VMEM)
HBM = pl.BlockSpec(memory_space=pltpu.HBM)
SMEM = pl.BlockSpec(memory_space=pltpu.SMEM)


def struct(shape, dtype):
    return jax.ShapeDtypeStruct(shape, dtype)


def call(body, name, outs, args, pieces=(), scratch=(), flops=0, moved=0, exps=0, limit=40):
    return pl.pallas_call(
        body,
        name=name,
        out_shape=outs,
        in_specs=[SMEM] + [VMEM] * (len(args) - 1) + [HBM] * len(pieces),
        out_specs=jax.tree.map(lambda _: VMEM, outs),
        scratch_shapes=scratch,
        cost_estimate=pl.CostEstimate(flops=flops, bytes_accessed=moved, transcendentals=exps),
        compiler_params=pltpu.CompilerParams(vmem_limit_bytes=limit * 2**20),
    )(*args, *pieces)


def columns(index, width):
    return pl.ds(pl.multiple_of(index * width, width), width)


def nt(a, b):
    return lax.dot_general(a, b, (((1,), (1,)), ((), ())), preferred_element_type=F32)


def tn(a, b):
    return lax.dot_general(a, b, (((0,), (0,)), ((), ())), preferred_element_type=F32)


def nn(a, b):
    return jnp.dot(a, b, preferred_element_type=F32)


def norm_rows(x, gain):
    wide = x.astype(F32)
    inverse = lax.rsqrt(jnp.mean(wide * wide, axis=-1, keepdims=True) + 1e-05)
    return (wide * inverse * gain).astype(BF16), inverse


def norm_into(inputs, gain, normed, inverse):
    step, row = 32, 0
    for x in inputs:
        for part in range(0, x.shape[0], step):
            out, inv = norm_rows(x[pl.ds(part, step), :], gain[...])
            normed[pl.ds(row, step), :] = out
            inverse[pl.ds(row, step), :] = jnp.broadcast_to(inv, (step, 128))
            row += step


def norm_ahead_body(pos, x, gain, normed, inverse):
    norm_into([x], gain, normed, inverse)


def norm_back_body(n_z, carry, pos, first, second, gain, partner, normed, inverse, own, right, left):
    norm_into([first, second], gain, normed, inverse)
    half, kv_width = first.shape[0], partner.shape[1]
    part = kv_width // 2

    def place(ref, row, away, begin=0, size=half):
        cols = columns(lax.rem(pos[0] + away, n_z), part)
        ref[pl.ds(row, size), :part] = normed[pl.ds(begin, size), cols]
        ref[pl.ds(row, size), part:] = normed[pl.ds(half + begin, size), cols]

    place(own, 0, 0)
    quarter = half // 2
    for ref, sign in ((right, 1), (left, -1)):
        place(ref, 0, n_z // 2, 0 if sign == 1 else quarter, quarter)
        row = quarter
        for away in range(n_z // 2 - 1, 0, -1):
            if away == carry:
                ref[pl.ds(row, partner.shape[0]), :] = partner[...]
                row += partner.shape[0]
            place(ref, row, (sign * away) % n_z)
            row += half


def rows_of(pos, place, n_z):
    dz, dy, part, parts = place
    owner = lax.rem(pos[0] + dz, n_z) * 2 + (pos[1] if dy == 0 else 1 - pos[1])
    return owner * parts + part


def fetch(pieces, held, sems):
    started, row = [], 0
    for i, (piece, (begin, size, place)) in enumerate(pieces):
        at = held.at[pl.ds(row, size), :]
        copy = pltpu.make_async_copy(piece.at[pl.ds(begin, size), :], at, sems.at[i])
        copy.start()
        started.append((place, at, copy))
        row += size
    return started


def held_rows(pieces):
    return sum(segment[1] for _, segment in pieces)


def project_body(places, n_z, begin, finish, pos, back, ahead, *refs):
    count = len(places)
    earlier, refs = (None, refs) if begin else (refs[0], refs[1:])
    pieces, outs = refs[:count], refs[count:-4]
    rows, total, held, sems = refs[-4:]
    started = fetch(list(zip(pieces, places)), held, sems)
    length = back.shape[0]
    rows[:length, :] = back[...]
    rows[length:, :] = ahead[...]
    if earlier is not None:
        total[...] = earlier[...]
    for i, (place, at, copy) in enumerate(started):
        copy.wait()
        part = nn(rows[:, columns(rows_of(pos, place, n_z), at.shape[0])], at[...])
        if i == 0 and begin:
            total[...] = part
        elif i < count - 1:
            total[...] += part
        elif finish:
            kv_back, kv_ahead = outs
            kv_back[...] = (total[:length, :] + part[:length, :]).astype(BF16)
            kv_ahead[...] = (total[length:, :] + part[length:, :]).astype(BF16)
        else:
            outs[0][...] = total[...] + part


def mask_of(doc):
    length = doc.shape[1]
    across = jnp.broadcast_to(doc.astype(F32), (length, length))
    query = lax.broadcasted_iota(jnp.int32, (length, length), 0)
    key = lax.broadcasted_iota(jnp.int32, (length, length), 1)
    return (query >= key) & (across == across.T)


def probs_of(query, key, mask):
    scores = jnp.where(mask, nt(query, key), F32(-1e30))
    highest = jnp.max(scores, axis=-1, keepdims=True)
    powers = jnp.exp2((scores - highest) * F32(SCALE * math.log2(math.e)))
    return powers * (1.0 / jnp.sum(powers, axis=-1, keepdims=True))


def head(i):
    return pl.ds(i * HEAD_DIM, HEAD_DIM)


def stacked(ref, group):
    return jnp.concatenate([ref[:, head(group * GROUP + j)] for j in range(GROUP)], axis=0)


def back_attention_body(pos, doc, normed, kv, cotangent, kv_cotan, score_grads):
    length = normed.shape[0]
    mask = jnp.concatenate([mask_of(doc[...])] * GROUP, axis=0)
    for group in range(KV_HEADS):
        key, value = kv[:, head(group)], kv[:, head(KV_HEADS + group)]
        query, grad = stacked(normed, group), stacked(cotangent, group)
        probs = probs_of(query, key, mask)
        prob_grad = nt(grad, value)
        centre = jnp.sum(probs * prob_grad, axis=-1, keepdims=True)
        score_grad = (probs * (prob_grad - centre) * F32(SCALE)).astype(BF16)
        for j in range(GROUP):
            score_grads[:, head(group * GROUP + j)] = score_grad[j * length : (j + 1) * length]
        kv_cotan[:, head(group)] = tn(score_grad, query).astype(BF16)
        kv_cotan[:, head(KV_HEADS + group)] = tn(probs.astype(BF16), grad).astype(BF16)


def park_body(pos, incoming, evicted, parked):
    half = evicted.shape[0]
    parked[0, 0] = incoming[:half, :]
    parked[1, 0] = evicted[...]


def ahead_attention_body(pos, doc, normed, kv, incoming, out):
    length = normed.shape[0]
    mask = jnp.concatenate([mask_of(doc[...])] * GROUP, axis=0)
    for group in range(KV_HEADS):
        probs = probs_of(stacked(normed, group), kv[:, head(group)], mask).astype(BF16)
        mixed = nn(probs, kv[:, head(KV_HEADS + group)])
        for j in range(GROUP):
            at = head(group * GROUP + j)
            total = incoming[:, at].astype(F32) + mixed[j * length : (j + 1) * length]
            out[0, :, at] = total.astype(BF16)


def input_grad_body(
    places, n_z, pos, score_grads, kv, kv_cotan, first, second, inverse, gain, cotangent, *refs
):
    pieces, (out, grads, held, sems) = refs[:-4], refs[-4:]
    started = fetch(list(zip(pieces, places)), held, sems)
    half, width = first.shape
    for group in range(KV_HEADS):
        key = kv[:, head(group)]
        for j in range(GROUP):
            at = head(group * GROUP + j)
            grads[:, at] = nn(score_grads[:, at], key)
    for _, _, copy in started:
        copy.wait()
    for place, at, _ in started:
        grads[:, columns(rows_of(pos, place, n_z), at.shape[0])] += nt(kv_cotan[...], at[...])
    step = 32
    for row in range(0, 2 * half, step):
        source, at = (first, row) if row < half else (second, row - half)
        wide = source[pl.ds(at, step), :].astype(F32)
        scaled = grads[pl.ds(row, step), :] * gain[...]
        moment = jnp.mean(scaled * wide, axis=-1, keepdims=True)
        inv = inverse[pl.ds(row, step), :1]
        total = cotangent[pl.ds(row, step), :].astype(F32) + inv * scaled - wide * (inv * inv * inv * moment)
        out[0, pl.ds(row, step), :] = total.astype(BF16)


def collect_body(moves, pos, *refs):
    sources, out, sems = refs[:-2], refs[-2], refs[-1]
    part = out.shape[1]
    copies = []
    for i, (source, begin, row, size, side) in enumerate(moves):
        copies.append(
            pltpu.make_async_copy(
                sources[source].at[pl.ds(begin, size), pl.ds(side * part, part)],
                out.at[pl.ds(row, size), :],
                sems.at[i],
            )
        )
        copies[-1].start()
    for copy in copies:
        copy.wait()


def kv_grad_body(other, pos, left, *refs):
    rights, out = refs[:-1], refs[-1]
    place = 1 - pos[1] if other else pos[1]
    right = jnp.concatenate([ref[...] for ref in rights], axis=0)
    out[...] = tn(left[:, columns(place, out.shape[0])], right).astype(out.dtype)


def add_body(pos, mine, theirs, out):
    out[0] = (mine[...] + theirs[...].astype(F32)).astype(BF16)


def section_permute(value, to):
    n = lax.axis_size("section")
    return lax.ppermute(value, "section", [(i, to(i) % n) for i in range(n)])


def dp_permute(value, dz=0, dy=0):
    n_z = lax.axis_size("dp") // 2
    pairs = [(i, ((i // 2 + dz) % n_z) * 2 + ((i % 2) ^ dy)) for i in range(2 * n_z)]
    return lax.ppermute(value, "dp", pairs)


def ring(block, n_z, ready, dy=0):
    got = [(block, (0, dy, 0, 1))]
    right = left = block
    for step in range(1, n_z // 2):
        right, left = dp_permute(right, dz=1), dp_permute(left, dz=-1)
        got += [(right, (n_z - step, dy, 0, 1)), (left, (step, dy, 0, 1))]
    half = block.shape[0] // 2
    right, left = tie(right, ready), tie(left, ready)
    got.append((dp_permute(right[:half], dz=1), (n_z // 2, dy, 0, 2)))
    got.append((dp_permute(left[half:], dz=-1), (n_z // 2, dy, 1, 2)))
    return got


def settle(value):
    return lax.optimization_barrier(value)


def tie(value, *others):
    return lax.optimization_barrier((value,) + others)[0]


def local(
    sent_forward, sent_backward, stash_halves, norm_gain, kv_weight, doc_forward, doc_backward
):
    n_dp = lax.axis_size("dp")
    n_z = n_dp // 2
    index = lax.axis_index("dp")
    pos = jnp.stack([index // 2, index % 2]).astype(jnp.int32)
    half, width = stash_halves.shape[2:]
    length = 2 * half
    weight = kv_weight[0]
    kv_width = weight.shape[1]

    last = lax.axis_size("section") - 1
    first = stash_halves[0, 0]
    piece_width = 2 * weight.shape[0]
    mid = weight.shape[0] // 2

    carry = 1

    def both(to_right, to_left):
        return dp_permute(to_right, dz=1), dp_permute(to_left, dz=-1)

    def over(pair):
        return tuple(settle(dp_permute(value, dy=1)) for value in pair)

    partner = settle(dp_permute(weight, dy=1))
    second = section_permute(tie(stash_halves[1, 0], partner), lambda i: last - i)
    rows, quarter = weight.shape[0], half // 2
    message = struct((quarter + (n_z // 2 - 1) * half + rows, kv_width), BF16)
    normed_back, inverse, own, *messages = call(
        functools.partial(norm_back_body, n_z, carry),
        "norm_back",
        [struct((length, width), BF16), struct((length, 128), F32), struct((half, kv_width), BF16)]
        + [message] * 2,
        [pos, first, second, norm_gain, partner],
        flops=6 * length * width,
        limit=12,
        moved=6 * length * width,
    )
    early = [(weight, (0, rows, (0, 0, 0, 1))), (partner, (0, rows, (0, 1, 0, 1)))]
    late, overs = [], []
    around = (weight, weight)
    for step in range(1, n_z // 2):
        around = both(*around)
        for value, dz in zip(around, (n_z - step, step)):
            early.append((value, (0, rows, (dz, 0, 0, 1))))
        if step < 3:
            around = tuple(tie(value, partner if step == 1 else inverse) for value in around)
        if step > carry:
            overs.append(over(around))
            for value, dz in zip(overs[-1], (n_z - step, step)):
                late.append((value, (0, rows, (dz, 1, 0, 1))))
        if step == 2:
            incoming = section_permute(tie(sent_forward, *around), lambda i: i + 1)[0]
    far = both(around[0][:mid], around[1][mid:])
    cotangent = section_permute(tie(sent_backward, *around), lambda i: i - 1)[0]
    overs.append(over(far))
    for dy, pair in enumerate((far, overs[-1])):
        for part, value in enumerate(pair):
            late.append((value, (0, mid, (n_z // 2, dy, part, 2))))
    evicted = section_permute(sent_forward[0, half:], lambda i: last - 1 - i)
    sources = [own]
    moves = [(0, 0, 0, half, 0), (0, 0, half, half, 1)]
    before = {3: [cotangent], 4: list(overs[-2])}
    for step in range(1, n_z // 2 + 1):
        size = quarter + (n_z // 2 - step) * half + (rows if step <= carry else 0)
        messages = both(*(tie(value[:size], *before.get(step, [])) for value in messages))
        if step == 2:
            second_step = messages
        for value, dz, part in zip(messages, (n_z - step, step), (0, 1)):
            if step <= carry:
                begin = quarter + (n_z // 2 - 1 - carry) * half
                late.append((value, (begin, rows, (dz, 1, 0, 1))))
            at = len(sources)
            sources.append(value)
            for side in range(2):
                if step == n_z // 2:
                    moves.append((at, 0, dz * length + side * half + part * quarter, quarter, side))
                else:
                    moves.append((at, value.shape[0] - half, dz * length + side * half, half, side))
    collected = call(
        functools.partial(collect_body, moves),
        "collect",
        struct((n_z * length, kv_width // 2), BF16),
        [pos],
        sources,
        scratch=[pltpu.SemaphoreType.DMA((len(moves),))],
        limit=6,
        moved=4 * length * width,
    )

    normed_ahead, _ = call(
        norm_ahead_body,
        "norm_ahead",
        [struct((length, width), BF16), struct((length, 128), F32)],
        [pos, incoming, norm_gain],
        flops=6 * length * width,
        limit=10,
        moved=4 * length * width,
    )


    def project(some, outs, total=None, finish=False):
        return call(
            functools.partial(project_body, tuple(q for _, q in some), n_z, total is None, finish),
            "project_late" if finish else "project_early",
            outs,
            [pos, normed_back, normed_ahead] + ([] if total is None else [total]),
            [p for p, _ in some],
            scratch=[
                pltpu.VMEM((2 * length, width), BF16),
                pltpu.VMEM((2 * length, kv_width), F32),
                pltpu.VMEM((held_rows(some), kv_width), BF16),
                pltpu.SemaphoreType.DMA((len(some),)),
            ],
            flops=2 * length * width * kv_width,
            limit=20,
            moved=width * kv_width,
        )

    total = project(early, struct((2 * length, kv_width), F32))
    kv_back, kv_ahead = project(
        late, [struct((length, kv_width), BF16)] * 2, tie(total, *second_step), True
    )
    kv_cotan, score_grads = call(
        back_attention_body,
        "back_attention",
        [struct((length, kv_width), BF16), struct((length, width), BF16)],
        [pos, doc_backward, normed_back, kv_back, cotangent],
        flops=10 * length * length * width,
        limit=12,
        moved=6 * length * width,
        exps=length * length * HEADS,
    )
    out = call(
        ahead_attention_body,
        "ahead_attention",
        struct((1, length, width), BF16),
        [pos, doc_forward, normed_ahead, kv_ahead, incoming],
        flops=4 * length * length * width,
        limit=12,
        moved=8 * length * width,
        exps=length * length * HEADS,
    )
    spread = ring(kv_cotan, n_z, out)
    parked = call(
        park_body,
        "park",
        struct((2, 1, half, width), BF16),
        [pos, incoming, evicted],
        limit=8,
        moved=4 * length * width,
    )
    input_grad = call(
        functools.partial(input_grad_body, tuple(q for _, q in early + late), n_z),
        "input_grad",
        struct((1, length, width), BF16),
        [pos, score_grads, kv_back, kv_cotan, first, second, inverse, norm_gain, cotangent],
        [p for p, _ in early + late],
        scratch=[
            pltpu.VMEM((length, width), F32),
            pltpu.VMEM((held_rows(early + late), kv_width), BF16),
            pltpu.SemaphoreType.DMA((len(early + late),)),
        ],
        flops=2 * length * width * (kv_width + length),
        limit=22,
        moved=2 * width * kv_width + 8 * length * width,
    )

    by_z = {}
    for piece, (dz, _, part, _) in spread:
        by_z.setdefault(dz, {})[part] = piece
    order = sorted(by_z)
    rights = [by_z[dz][part] for dz in order for part in sorted(by_z[dz])]
    own_rows = weight.shape[0]

    def kv_part(other, dtype):
        return call(
            functools.partial(kv_grad_body, other),
            "kv_grad_other" if other else "kv_grad_own",
            struct((own_rows, kv_width), dtype),
            [pos, collected] + rights,
            flops=2 * own_rows * kv_width * length * n_z,
            limit=12,
            moved=2 * length * n_z * (kv_width + own_rows),
        )

    theirs = dp_permute(kv_part(True, BF16), dy=1)
    mine = kv_part(False, F32)
    kv_grad = call(
        add_body,
        "kv_add",
        struct((1, own_rows, kv_width), BF16),
        [pos, mine, theirs],
        flops=own_rows * kv_width,
        limit=6,
        moved=8 * own_rows * kv_width,
    )
    return out, input_grad, parked, kv_grad


def solution(mesh):
    return jax.shard_map(
        local,
        mesh=mesh,
        in_specs=(
            P("section", "dp", None),
            P("section", "dp", None),
            P(None, "section", "dp", None),
            P("section", None),
            P("section", "dp", None),
            P("section", "dp"),
            P("section", "dp"),
        ),
        out_specs=(
            P("section", "dp", None),
            P("section", "dp", None),
            P(None, "section", "dp", None),
            P("section", "dp", None),
        ),
        check_vma=False,
    )
```
